32 devices in a mesh: section: 2 (over y), row: 4 (over z), tp: 4 (over x, core).
Axes of the slice: x: 2, y: 2, z: 4, core: 2. Of those that a mesh axis runs over, the one named last changes fastest.
Arguments:
- section_feeds: bfloat16 [2, 2, 128, 8192], P('section', None, None, 'row'), may hold values from -6 to 6
- norm_gain: float32 [2, 8192], P('section', 'row'), may hold values from 0.1 to 1.9
- up_weight: bfloat16 [2, 8192, 32768], P('section', 'row', 'tp'), may hold values from -0.0625 to 0.0625
- down_weight: bfloat16 [2, 32768, 8192], P('section', 'tp', 'row'), may hold values from -0.03125 to 0.03125
Outputs:
- section_ends: bfloat16 [2, 2, 128, 8192], P('section', None, None, 'row')
The draws below stay inside these ranges and needn't reach their ends.
All inputs are finite; a program needn't handle non-finite values.
Results may differ from the reference program's by a relative error of at most 0.011.
Values may be sent and summed in bfloat16 or wider, within the bound.
A program may use at most 192 MiB of HBM per device.

```python
import jax
import jax.numpy as jnp
from jax import lax

D = 8192
FF = 32768
TOK = 128
MICRO = 2


def block_levels(own_key, extent, split, smallest, largest):
    def one(axis_at, shards_of):
        draws = jax.random.uniform(jax.random.fold_in(jax.random.fold_in(own_key, 6), axis_at), (shards_of,), jnp.float32, smallest / len(split), largest / len(split))
        return jnp.repeat(jnp.exp(draws), extent[axis_at] // shards_of).reshape((-1,) + (1,) * (len(extent) - axis_at - 1))

    level = one(*split[0])
    for cut in split[1:]:
        level = level * one(*cut)
    return level


def gaussian(rng, extent, width, limit, split=(), dtype=jnp.bfloat16):
    loudness = block_levels(rng, extent, split, -0.22, 0.18) if split else 1.0
    values = jax.random.normal(rng, extent, jnp.float32) * width * loudness
    return jnp.minimum(jnp.maximum(values, -limit), limit).astype(dtype)


def setup_inputs(seed: int = 0) -> dict:
    seeds = jax.random.split(jax.random.key(seed), 5)
    section_feeds = gaussian(seeds[0], (2, MICRO, TOK, D), 1.0, 6.0, ((0, 2), (3, 4)))
    norm_gain = jnp.clip(1.0 + 0.18 * jax.random.normal(seeds[1], (2, D), jnp.float32), 0.1, 1.9)
    up_weight = gaussian(seeds[2], (2, D, FF), D ** -0.5, 0.0625, ((0, 2), (1, 4), (2, 4)))
    down_weight = gaussian(seeds[3], (2, FF, D), FF ** -0.5, 0.03125, ((0, 2), (1, 4), (2, 4)))
    return dict(section_feeds=section_feeds, norm_gain=norm_gain, up_weight=up_weight, down_weight=down_weight)


epsilon = 1e-05
gelu_coeff = 0.7978845608028654

def gelu_value(inputs):
    inner = gelu_coeff * (inputs + 0.044715 * inputs * inputs * inputs)
    return 0.5 * inputs * (1.0 + jnp.tanh(inner))

def gelu_slope(inputs):
    inner = gelu_coeff * (inputs + 0.044715 * inputs * inputs * inputs)
    tangent = jnp.tanh(inner)
    return 0.5 * (1.0 + tangent) + 0.5 * inputs * (1.0 - tangent * tangent) * gelu_coeff * (1.0 + 3.0 * 0.044715 * inputs * inputs)

def layer_forward(inputs, gain_row, up_matrix, down_matrix):
    values = inputs.astype(jnp.float32)
    row_mean = lax.optimization_barrier(jnp.sum(values, axis=1)) / D
    variance = lax.optimization_barrier(jnp.sum(values * values, axis=1)) / D - row_mean * row_mean
    inv_std = lax.rsqrt(variance + epsilon)
    normed = (values - row_mean[:, None]) * inv_std[:, None]
    scaled = (normed * gain_row.astype(jnp.float32)[None, :]).astype(jnp.bfloat16)
    hidden_pre = jnp.dot(scaled, up_matrix, preferred_element_type=jnp.float32)
    hidden = gelu_value(hidden_pre).astype(jnp.bfloat16)
    branch = jnp.dot(hidden, down_matrix, preferred_element_type=jnp.float32)
    return ((values + branch).astype(jnp.bfloat16), (normed, inv_std, hidden_pre))

def layer_backward(incoming, gain_row, up_matrix, down_matrix, saved):
    normed, inv_std, hidden_pre = saved
    hidden_grad = jnp.dot(incoming, down_matrix.T, preferred_element_type=jnp.float32)
    pre_grad = (hidden_grad * gelu_slope(hidden_pre)).astype(jnp.bfloat16)
    normed_grad = jnp.dot(pre_grad, up_matrix.T, preferred_element_type=jnp.float32) * gain_row.astype(jnp.float32)[None, :]
    first_mean = lax.optimization_barrier(jnp.sum(normed_grad, axis=1)) / D
    second_mean = lax.optimization_barrier(jnp.sum(normed_grad * normed, axis=1)) / D
    result = incoming.astype(jnp.float32) + inv_std[:, None] * (normed_grad - first_mean[:, None] - normed * second_mean[:, None])
    return result.astype(jnp.bfloat16)

def reference(section_feeds, norm_gain, up_weight, down_weight):
    outputs = []
    gradients = []
    for micro_index in range(MICRO):
        middle, saved_first = layer_forward(section_feeds[0, micro_index], norm_gain[0], up_weight[0], down_weight[0])
        final, saved_second = layer_forward(middle, norm_gain[1], up_weight[1], down_weight[1])
        back_grad = layer_backward(section_feeds[1, micro_index], norm_gain[1], up_weight[1], down_weight[1], saved_second)
        gradients.append(layer_backward(back_grad, norm_gain[0], up_weight[0], down_weight[0], saved_first))
        outputs.append(final)
    return jnp.stack([jnp.stack(gradients), jnp.stack(outputs)])
```

```python
import jax
import jax.numpy as jnp
from jax import lax
from jax.sharding import PartitionSpec as P

D = 8192


epsilon = 1e-05
gelu_coeff = 0.7978845608028654


def shifted(array, axis, by):
    devices = lax.axis_size(axis)
    pairs = [(i, i + by) for i in range(devices) if 0 <= i + by < devices]
    return lax.ppermute(array, axis, pairs)


def gelu_value(inputs):
    inner = gelu_coeff * (inputs + 0.044715 * inputs * inputs * inputs)
    return 0.5 * inputs * (1.0 + jnp.tanh(inner))


def gelu_slope(inputs):
    inner = gelu_coeff * (inputs + 0.044715 * inputs * inputs * inputs)
    tangent = jnp.tanh(inner)
    return 0.5 * (1.0 + tangent) + 0.5 * inputs * (1.0 - tangent * tangent) * gelu_coeff * (
        1.0 + 3.0 * 0.044715 * inputs * inputs
    )


def row_pair(first_arr, second_arr):
    return lax.psum((jnp.sum(first_arr, axis=1), jnp.sum(second_arr, axis=1)), "row")


def body(section_feeds, norm_gain, up_weight, down_weight):
    up_local = up_weight[0]
    down_local = down_weight[0]
    gain_row = norm_gain[0]
    feeds_local = section_feeds[0]
    micro_count = feeds_local.shape[0]
    is_first = lax.axis_index("section") == 0

    def hidden_total(term):
        return lax.psum(term.astype(jnp.bfloat16), "row").astype(jnp.float32)

    def feature_total(term):
        return lax.psum(term.astype(jnp.bfloat16), "tp").astype(jnp.float32)

    def up_term(scaled):
        return lax.dot_general(
            up_local, scaled, (((0,), (1,)), ((), ())), preferred_element_type=jnp.float32
        )

    def back_term(incoming):
        return lax.dot_general(
            down_local, incoming, (((1,), (1,)), ((), ())), preferred_element_type=jnp.float32
        )

    def forward_fold(activated):
        return lax.dot_general(
            activated, down_local, (((0,), (0,)), ((), ())), preferred_element_type=jnp.float32
        )

    def backward_fold(pre_grad):
        return lax.dot_general(
            pre_grad, up_local, (((0,), (1,)), ((), ())), preferred_element_type=jnp.float32
        )

    def normalise(inputs):
        values = inputs.astype(jnp.float32)
        row_sum, squares = row_pair(values, values * values)
        row_mean = row_sum / D
        variance = squares / D - row_mean * row_mean
        inv_std = lax.rsqrt(variance + epsilon)
        normed = (values - row_mean[:, None]) * inv_std[:, None]
        return (normed * gain_row[None, :]).astype(jnp.bfloat16), normed, inv_std

    def activate(hidden_pre):
        return gelu_value(hidden_pre).astype(jnp.bfloat16)

    def slope_times(hidden_grad, hidden_pre):
        return (hidden_grad * gelu_slope(hidden_pre)).astype(jnp.bfloat16)

    def residual(inputs, branch):
        return (inputs.astype(jnp.float32) + branch).astype(jnp.bfloat16)

    def input_grad(incoming, folded, normed, inv_std):
        normed_grad = folded * gain_row[None, :]
        first_sum, second_sum = row_pair(normed_grad, normed_grad * normed)
        result = incoming.astype(jnp.float32) + inv_std[:, None] * (
            normed_grad - (first_sum / D)[:, None] - normed * (second_sum / D)[:, None]
        )
        return result.astype(jnp.bfloat16)

    feeds = [feeds_local[index] for index in range(micro_count)]
    last = micro_count - 1
    outputs = [None] * micro_count
    grads = [None] * micro_count
    saved = [None] * micro_count
    early_grad = None
    middle = None
    back = None

    scaled, normed, inv_std = normalise(feeds[0])
    total = hidden_total(
        lax.cond(is_first, lambda: up_term(scaled), lambda: back_term(feeds[0]))
    )
    early_grad = total
    first_saved = [(normed, inv_std, total)]
    middle = residual(feeds[0], feature_total(forward_fold(activate(total))))
    middle = shifted(middle, "section", 1)

    for index in range(micro_count):
        if index < last:
            inputs = jnp.where(is_first, feeds[index + 1], middle)
            scaled, normed, inv_std = normalise(inputs)
            total = hidden_total(up_term(scaled))
            first_saved.append((normed, inv_std, total))
            late_saved = (normed, inv_std, total)
            produced = residual(inputs, feature_total(forward_fold(activate(total))))
            outputs[index] = produced
            middle = shifted(produced, "section", 1)
        else:
            scaled, normed, inv_std = normalise(middle)
            late_saved = (normed, inv_std, None)
            incoming = back
            total = hidden_total(
                lax.cond(is_first, lambda: back_term(incoming), lambda: up_term(scaled))
            )
            late_saved = (normed, inv_std, total)
            prior_normed, prior_inv, prior_pre = first_saved[index - 1]
            folded = feature_total(
                lax.cond(
                    is_first,
                    lambda: backward_fold(slope_times(total, prior_pre)),
                    lambda: forward_fold(activate(total)),
                )
            )
            outputs[index] = residual(middle, folded)
            grads[index - 1] = input_grad(incoming, folded, prior_normed, prior_inv)
            early_grad = hidden_total(back_term(feeds[index]))
        normed, inv_std, hidden_pre = late_saved
        folded = feature_total(backward_fold(slope_times(early_grad, hidden_pre)))
        back = shifted(input_grad(feeds[index], folded, normed, inv_std), "section", -1)

    normed, inv_std, hidden_pre = first_saved[last]
    total = hidden_total(back_term(back))
    folded = feature_total(backward_fold(slope_times(total, hidden_pre)))
    grads[last] = input_grad(back, folded, normed, inv_std)
    ends_local = jnp.stack(
        [jnp.where(is_first, grads[index], outputs[index]) for index in range(micro_count)]
    )
    return ends_local[None]


def solution(mesh):
    placed = (
        P("section", None, None, "row"),
        P("section", "row"),
        P("section", "row", "tp"),
        P("section", "tp", "row"),
    )
    return jax.shard_map(
        body, mesh=mesh, in_specs=placed, out_specs=P("section", None, None, "row"), check_vma=False
    )
```
